32 devices in a mesh: ctx: 16 (over z, y, core), ch: 2 (over x).
Axes of the slice: x: 2, y: 2, z: 4, core: 2. Of those that a mesh axis runs over, the one named last changes fastest.
Arguments:
- grad_out: bfloat16 [2, 32, 65536], P(None, 'ch', 'ctx'), may hold values from -6 to 6
- inputs: bfloat16 [2, 32, 65536], P(None, 'ch', 'ctx'), may hold values from -6 to 6
- gates: bfloat16 [2, 32, 65536], P(None, 'ch', 'ctx'), may hold values from -6 to 6
- residues: float32 [512], P(('ctx', 'ch')), may hold values from -1.5 to 1.5
- rates: float32 [512], P(('ctx', 'ch')), as said below
- skip: float32 [32], P('ch'), may hold values from 0.5 to 1.5
Outputs:
- d_input: bfloat16 [2, 32, 65536], P(None, 'ch', 'ctx')
- d_gate: bfloat16 [2, 32, 65536], P(None, 'ch', 'ctx')
- d_residues: float32 [512], P(('ctx', 'ch'))
- d_log_rates: float32 [512], P(('ctx', 'ch'))
- d_skip: float32 [32], P('ch')
The draws below stay inside these ranges and needn't reach their ends.
Inputs may be any that keep to these rules, and one draw needn't show every extreme that they name: `rates`: every rate is positive and at most 1 / 40.
All inputs are finite; a program needn't handle non-finite values.
Results may differ from the reference program's by a relative error of at most 0.01.
Values may be sent and summed in bfloat16 or wider, within the bound.
A program may use at most 128 MiB of HBM per device.

```python
import jax
import jax.numpy as jnp
from jax import lax

SEQS = 2
ORDER = 16
C = 32
LENGTH = 65536


def rate_values(key, slowest, fastest):
    uniform_draw = jax.random.uniform(jax.random.fold_in(key, 11), (C * ORDER,), jnp.float32)
    return jnp.exp(jnp.log(slowest) + uniform_draw * (jnp.log(fastest) - jnp.log(slowest)))


def draw_rates(key, part):
    key = jax.random.fold_in(key, 3)
    return rate_values(key, 1.0 / LENGTH, 1.0 / 40.0)


def block_levels(own_key, shape, shards, least, high):
    loudness = 1.0
    for axis_at, shards_of in shards:
        heights = jax.random.uniform(jax.random.fold_in(jax.random.fold_in(own_key, 6), axis_at), (shards_of,), jnp.float32, least / len(shards), high / len(shards))
        loudness = loudness * jnp.repeat(jnp.exp(heights), shape[axis_at] // shards_of).reshape((-1,) + (1,) * (len(shape) - 1 - axis_at))
    return loudness


def bell_draw(key, dims, width, limit, split=(), kind=jnp.bfloat16):
    result = jax.random.normal(key, dims, jnp.float32) * width
    if len(split) > 0:
        result = block_levels(key, dims, split, -0.22, 0.18) * result
    return jnp.clip(result, min=-limit, max=limit).astype(kind)


def setup_inputs(seed: int = 0) -> dict:
    key_of = jax.random.split(jax.random.key(seed), 7)
    return {
        "grad_out": bell_draw(key_of[0], (SEQS, C, LENGTH), 1.0, 6.0, ((1, 2), (2, 16))),
        "inputs": bell_draw(key_of[1], (SEQS, C, LENGTH), 1.0, 6.0, ((1, 2), (2, 16))),
        "gates": bell_draw(key_of[2], (SEQS, C, LENGTH), 1.0, 6.0, ((1, 2), (2, 16))),
        "residues": bell_draw(key_of[3], (C * ORDER,), 0.25, 1.5, ((0, 32),), jnp.float32),
        "rates": draw_rates(jax.random.fold_in(key_of[6], 71), 0),
        "skip": jnp.clip(0.5 + 1.0 * jax.random.uniform(key_of[5], (C,), jnp.float32) ** block_levels(key_of[5], (C,), ((0, 2),), -0.2, 0.2), 0.5, 1.5),
    }


def reference(grad_out, inputs, gates, residues, rates, skip):
    positions = jnp.arange(LENGTH).astype(jnp.float32)
    padded_length = 2 * LENGTH
    factor = (SEQS * LENGTH) ** (-0.5)
    res_table = residues.reshape(C, ORDER)
    rate_table = rates.reshape(C, ORDER)

    def channel(operands):
        grad_rows, input_rows, gate_rows, residue, rate_row, gain = operands
        decays = jnp.exp(-rate_row[:, None] * positions[None, :])
        amplitude = jnp.sqrt(2.0 * rate_row)
        kernel = lax.optimization_barrier(jnp.sum((residue * amplitude)[:, None] * decays, axis=0))
        input_wide = input_rows.astype(jnp.float32)
        input_freq = jnp.fft.rfft(input_wide, n=padded_length, axis=-1)
        kernel_freq = jnp.fft.rfft(kernel, n=padded_length)
        convolved = jnp.fft.irfft(input_freq * kernel_freq[None, :], n=padded_length, axis=-1)[:, :LENGTH]
        conv_out = (convolved + gain * input_wide).astype(jnp.bfloat16)
        grad_wide = grad_rows.astype(jnp.float32)
        grad_mid = (grad_wide * gate_rows.astype(jnp.float32)).astype(jnp.bfloat16)
        mid_wide = lax.optimization_barrier(grad_mid).astype(jnp.float32)
        d_gate = (grad_wide * lax.optimization_barrier(conv_out).astype(jnp.float32)).astype(jnp.bfloat16)
        mid_freq = jnp.fft.rfft(mid_wide, n=padded_length, axis=-1)
        correlated = jnp.fft.irfft(jnp.conj(kernel_freq)[None, :] * mid_freq, n=padded_length, axis=-1)[:, :LENGTH]
        d_input = (correlated + gain * mid_wide).astype(jnp.bfloat16)
        lagged = lax.optimization_barrier(jnp.sum(jnp.fft.irfft(jnp.conj(input_freq) * mid_freq, n=padded_length, axis=-1)[:, :LENGTH], axis=0))
        weighted = jnp.dot(decays, lagged, precision=lax.Precision.HIGHEST)
        moment = jnp.dot(decays, positions * lagged, precision=lax.Precision.HIGHEST)
        d_res = factor * amplitude * weighted
        d_log = factor * residue * amplitude * (0.5 * weighted - rate_row * moment)
        d_gain = factor * jnp.sum(mid_wide * input_wide)
        return (d_input, d_gate, d_res, d_log, d_gain)
    results = lax.map(channel, (jnp.swapaxes(grad_out, 0, 1), jnp.swapaxes(inputs, 0, 1), jnp.swapaxes(gates, 0, 1), res_table, rate_table, skip))
    return (jnp.swapaxes(results[0], 0, 1), jnp.swapaxes(results[1], 0, 1), results[2].reshape(-1), results[3].reshape(-1), results[4])
```

```python
import functools

import jax
import jax.numpy as jnp
from jax import lax
from jax.experimental import pallas as pl
from jax.experimental.pallas import tpu as pltpu
from jax.sharding import PartitionSpec as P

ORDER = 16
CHUNK = 128
f32 = jnp.float32
bf16 = jnp.bfloat16
NT = (((1,), (1,)), ((), ()))
TN = (((0,), (0,)), ((), ()))
NN = (((1,), (0,)), ((), ()))


def dot(a, b, dims):
    return lax.dot_general(a, b, dims, preferred_element_type=f32)


def iota(shape, axis):
    return lax.broadcasted_iota(jnp.int32, shape, axis)


def turn(v, shift):
    shift = shift % CHUNK
    return v if shift == 0 else pltpu.roll(v, shift, axis=1)


def skew8(v, sign):
    row = iota((8, CHUNK), 0)
    for bit in (1, 2, 4):
        v = jnp.where((row // bit) % 2 == 1, turn(v, sign * bit), v)
    return v


def body(devs, grad_ref, input_ref, gate_ref, rcol_ref, gcol_ref, rlane_ref, skip_ref,
         din_ref, dgate_ref, out_ref,
         xs, gs, p0, p1, g0, g1, ys, zs, wl, send, slots, send_sem, recv_sem):
    seqs, chans, span = grad_ref.shape
    rows = seqs * chans
    count = span // CHUNK
    me = lax.axis_index("ctx")
    barrier = pltpu.get_barrier_semaphore()
    for d in range(1, devs):
        pl.semaphore_signal(barrier, inc=1, device_id={"ctx": lax.rem(me + d, devs)},
                            device_id_type=pl.DeviceIdType.MESH)

    lane = iota((ORDER, CHUNK), 1).astype(f32)
    rest = jnp.zeros((CHUNK - ORDER, CHUNK), bf16)

    for k in range(count):
        at = pl.ds(k * CHUNK, CHUNK)
        to = pl.ds(k * rows, rows)
        xs[to, :] = input_ref[:, :, at].astype(f32).reshape(rows, CHUNK)
        mid = grad_ref[:, :, at].astype(f32) * gate_ref[:, :, at].astype(f32)
        gs[to, :] = mid.astype(bf16).astype(f32).reshape(rows, CHUNK)

    def pick(c):
        return pl.ds(c, count * seqs, stride=chans)

    for c in range(chans):
        rc = rcol_ref[c * ORDER:(c + 1) * ORDER, :]
        x = xs[pick(c), :].astype(bf16)
        g = gs[pick(c), :].astype(bf16)
        dec = jnp.exp(-rc * lane)
        eg = jnp.exp(-rc * (lane + 1.0))
        ep = jnp.exp(-rc * (CHUNK - 1.0 - lane))
        wx = jnp.concatenate([ep.astype(bf16), rest, (ep * (CHUNK - 1.0 - lane)).astype(bf16), rest], 0)
        wg = jnp.concatenate([eg.astype(bf16), rest, (eg * (lane + 1.0)).astype(bf16), rest], 0)
        wd = jnp.concatenate([dec.astype(bf16), rest, (dec * lane).astype(bf16), rest], 0)
        px = dot(x, wx, NT)
        p0[pick(c), :] = px[:, :CHUNK]
        p1[pick(c), :] = px[:, CHUNK:]
        pg = dot(g, wg, NT)
        g0[pick(c), :] = pg[:, :CHUNK]
        g1[pick(c), :] = pg[:, CHUNK:]
        outer = dot(x, g, TN)
        acc = jnp.zeros((8, CHUNK), f32)
        for q in range(CHUNK // 8):
            piece = outer[8 * q:8 * q + 8]
            keep = iota((8, CHUNK), 1) >= iota((8, CHUNK), 0) + 8 * q
            acc = acc + turn(jnp.where(keep, piece, 0.0), -8 * q)
        acc = skew8(acc, -1)
        high = acc.astype(bf16)
        low = (acc - high.astype(f32)).astype(bf16)
        local = dot(high, wd, NT) + dot(low, wd, NT)
        local = jnp.sum(local, axis=0, keepdims=True)
        wl[0, c:c + 1, :] = local[:, :CHUNK]
        wl[1, c:c + 1, :] = local[:, CHUNK:]
        wl[2, c:c + 1, :] = jnp.sum(acc, axis=0, keepdims=True)

    rl = rlane_ref[...]
    fade = jnp.exp(-rl * CHUNK)
    zero = jnp.zeros((rows, CHUNK), f32)
    s0, s1, weighted, moment = zero, zero, zero, zero
    for k in range(count):
        to = pl.ds(k * rows, rows)
        a0, a1, b0, b1 = p0[to, :], p1[to, :], g0[to, :], g1[to, :]
        weighted = weighted + b0 * s0
        moment = moment + b1 * s0 + b0 * s1
        p0[to, :] = s0
        s0, s1 = fade * s0 + a0, fade * (s1 + CHUNK * s0) + a1
    r0, r1 = zero, zero
    for k in reversed(range(count)):
        to = pl.ds(k * rows, rows)
        b0, b1 = g0[to, :], g1[to, :]
        g0[to, :] = r0
        r0, r1 = fade * r0 + b0, fade * (r1 + CHUNK * r0) + b1

    def pack(v):
        total = v[0:8]
        for q in range(1, rows // 8):
            total = total + turn(v[8 * q:8 * q + 8], ORDER * q)
        return total

    def unpack(v):
        keep = iota((8, CHUNK), 1) < ORDER
        return jnp.concatenate([jnp.where(keep, turn(v, -ORDER * q), 0.0) for q in range(rows // 8)], 0)

    send[0] = pack(s0)
    send[1] = pack(r0)
    pl.semaphore_wait(barrier, devs - 1)
    copies = []
    for d in range(1, devs):
        copy = pltpu.make_async_remote_copy(
            src_ref=send.at[(me + d) // devs],
            dst_ref=slots.at[me],
            send_sem=send_sem.at[d],
            recv_sem=recv_sem.at[d],
            device_id={"ctx": lax.rem(me + d, devs)},
            device_id_type=pl.DeviceIdType.MESH,
        )
        copy.start()
        copies.append(copy)

    for c in range(chans):
        rc = rcol_ref[c * ORDER:(c + 1) * ORDER, :]
        gc = gcol_ref[c * ORDER:(c + 1) * ORDER, :]
        kern = jnp.sum(gc * jnp.exp(-rc * lane), axis=0, keepdims=True)
        base = skew8(jnp.broadcast_to(kern, (8, CHUNK)), 1)
        parts = []
        for q in range(CHUNK // 8):
            keep = iota((8, CHUNK), 1) >= iota((8, CHUNK), 0) + 8 * q
            parts.append(jnp.where(keep, turn(base, 8 * q), 0.0))
        toep = jnp.concatenate(parts, 0).astype(bf16)
        x = xs[pick(c), :]
        g = gs[pick(c), :]
        sk = skip_ref[c:c + 1, :]
        ys[pick(c), :] = dot(x.astype(bf16), toep, NN) + sk * x
        zs[pick(c), :] = dot(g.astype(bf16), toep, NT) + sk * g

    for copy in copies:
        copy.wait()
    rp = pack(rl)
    s_in, sn_in, r_in = (jnp.zeros((8, CHUNK), f32) for _ in range(3))
    for d in range(1, devs):
        v = slots[lax.rem(me + devs - d, devs)]
        left = jnp.where(me >= d, 1.0, 0.0)
        term = left * jnp.exp(-rp * (span * (d - 1.0))) * v
        s_in = s_in + term
        sn_in = sn_in + (span * (d - 1.0)) * term
        r_in = r_in + (1.0 - left) * jnp.exp(-rp * (span * (devs - d - 1.0))) * v
    s_in, sn_in, r_in = unpack(s_in), unpack(sn_in), unpack(r_in)
    weighted = weighted + r0 * s_in
    moment = moment + r1 * s_in + r0 * sn_in + s1 * r_in
    for s in range(seqs):
        wl[0] = wl[0] + weighted[s * chans:(s + 1) * chans]
        wl[1] = wl[1] + moment[s * chans:(s + 1) * chans]
    out_ref[...] = wl[...]

    for k in range(count):
        to = pl.ds(k * rows, rows)
        p0[to, :] = p0[to, :] + s_in
        s_in = s_in * fade
    for k in reversed(range(count)):
        to = pl.ds(k * rows, rows)
        g0[to, :] = g0[to, :] + r_in
        r_in = r_in * fade

    for c in range(chans):
        rc = rcol_ref[c * ORDER:(c + 1) * ORDER, :]
        gc = gcol_ref[c * ORDER:(c + 1) * ORDER, :]
        we = jnp.concatenate([(gc * jnp.exp(-rc * (lane + 1.0))).astype(bf16), rest], 0)
        wp = jnp.concatenate([(gc * jnp.exp(-rc * (CHUNK - 1.0 - lane))).astype(bf16), rest], 0)
        ys[pick(c), :] = ys[pick(c), :] + dot(p0[pick(c), :].astype(bf16), we, NN)
        zs[pick(c), :] = zs[pick(c), :] + dot(g0[pick(c), :].astype(bf16), wp, NN)

    for k in range(count):
        at = pl.ds(k * CHUNK, CHUNK)
        to = pl.ds(k * rows, rows)
        conv = ys[to, :].astype(bf16).astype(f32).reshape(seqs, chans, CHUNK)
        dgate_ref[:, :, at] = (grad_ref[:, :, at].astype(f32) * conv).astype(bf16)
        din_ref[:, :, at] = zs[to, :].astype(bf16).reshape(seqs, chans, CHUNK)


def shards(grad_out, inputs, gates, residues, rates, skip):
    seqs, chans, span = grad_out.shape
    devs = lax.axis_size("ctx")
    group = lax.axis_index("ch")
    tables = lax.all_gather(jnp.stack([residues, rates]), ("ctx", "ch"), axis=1, tiled=True)
    total = tables.shape[1] // ORDER
    tables = tables.reshape(2, total, ORDER)
    own = lax.dynamic_slice_in_dim(tables, group * chans, chans, axis=1)
    res, rate = own[0], own[1]
    amp = jnp.sqrt(2.0 * rate)
    wide = (chans * ORDER, CHUNK)
    rcol = jnp.broadcast_to(rate.reshape(-1, 1), wide)
    gcol = jnp.broadcast_to((res * amp).reshape(-1, 1), wide)
    rlane = jnp.pad(jnp.tile(rate, (seqs, 1)), ((0, 0), (0, CHUNK - ORDER)))
    skips = jnp.broadcast_to(skip[:, None], (chans, CHUNK))
    elems = span // CHUNK * seqs * chans
    big = pltpu.VMEM((elems, CHUNK), f32)
    vmem = pl.BlockSpec(memory_space=pltpu.VMEM)
    d_input, d_gate, sums = pl.pallas_call(
        functools.partial(body, devs),
        out_shape=(
            jax.ShapeDtypeStruct(grad_out.shape, bf16),
            jax.ShapeDtypeStruct(grad_out.shape, bf16),
            jax.ShapeDtypeStruct((3, chans, CHUNK), f32),
        ),
        in_specs=[vmem] * 7,
        out_specs=(vmem, vmem, vmem),
        scratch_shapes=[big] * 8 + [
            pltpu.VMEM((3, chans, CHUNK), f32),
            pltpu.VMEM((2, 8, CHUNK), f32),
            pltpu.VMEM((devs, 8, CHUNK), f32),
            pltpu.SemaphoreType.DMA((devs,)),
            pltpu.SemaphoreType.DMA((devs,)),
        ],
        compiler_params=pltpu.CompilerParams(
            collective_id=0, has_side_effects=True, vmem_limit_bytes=40 * 2 ** 20
        ),
    )(grad_out, inputs, gates, rcol, gcol, rlane, skips)
    factor = (seqs * span * devs) ** (-0.5)
    weighted, moment = sums[0, :, :ORDER], sums[1, :, :ORDER]
    d_res = factor * amp * weighted
    d_log = factor * res * amp * (0.5 * weighted - rate * moment)
    spread = jnp.zeros((2, total, ORDER), f32)
    spread = lax.dynamic_update_slice_in_dim(spread, jnp.stack([d_res, d_log]), group * chans, axis=1)
    spread = lax.psum_scatter(spread.reshape(2, -1), ("ctx", "ch"), scatter_dimension=1, tiled=True)
    d_skip = lax.psum(factor * sums[2, :, 0], "ctx")
    return (d_input, d_gate, spread[0], spread[1], d_skip)


def solution(mesh):
    wide = P(None, "ch", "ctx")
    flat = P(("ctx", "ch"))
    return jax.shard_map(
        shards,
        mesh=mesh,
        in_specs=(wide, wide, wide, flat, flat, P("ch")),
        out_specs=(wide, wide, flat, flat, P("ch")),
        check_vma=False,
    )
```

```python
import functools

import jax
import jax.numpy as jnp
from jax import lax
from jax.experimental import pallas as pl
from jax.experimental.pallas import tpu as pltpu
from jax.sharding import PartitionSpec as P

ORDER = 16
CHUNK = 128
f32 = jnp.float32
bf16 = jnp.bfloat16
NT = (((1,), (1,)), ((), ()))
TN = (((0,), (0,)), ((), ()))
NN = (((1,), (0,)), ((), ()))


def dot(a, b, dims):
    return lax.dot_general(a, b, dims, preferred_element_type=f32)


def iota(shape, axis):
    return lax.broadcasted_iota(jnp.int32, shape, axis)


def turn(v, shift):
    shift = shift % CHUNK
    return v if shift == 0 else pltpu.roll(v, shift, axis=1)


def skew8(v, sign):
    row = iota((8, CHUNK), 0)
    for bit in (1, 2, 4):
        v = jnp.where((row // bit) % 2 == 1, turn(v, sign * bit), v)
    return v


def spot(flat, groups):
    return {"ctx": flat // groups, "ch": lax.rem(flat, groups)}


def body(devs, groups, held, factor, grad_ref, input_ref, gate_ref, pack_ref,
         din_ref, dgate_ref, out_ref,
         xs, gs, p0, p1, g0, g1, ys, zs, wl, lags, rcols, gcols, tabs, send, slots,
         row, rows_in, parts_out, parts_in,
         send_sem, recv_sem, row_send, row_recv, part_send, part_recv):
    seqs, chans, span = grad_ref.shape
    rows = seqs * chans
    count = span // CHUNK
    me = lax.axis_index("ctx")
    group = lax.axis_index("ch")
    flat = me * groups + group
    everyone = devs * groups
    home = flat // devs
    place = lax.rem(flat, devs)
    local = home == group
    pieces = ORDER // held
    barrier = pltpu.get_barrier_semaphore()

    @pl.loop(1, everyone)
    def _(d):
        pl.semaphore_signal(barrier, inc=1, device_id=spot(lax.rem(flat + d, everyone), groups),
                            device_id_type=pl.DeviceIdType.MESH)

    def row_copy(e):
        return pltpu.make_async_remote_copy(
            src_ref=row.at[0], dst_ref=rows_in.at[place],
            send_sem=row_send.at[e], recv_sem=row_recv.at[place],
            device_id={"ctx": e, "ch": home}, device_id_type=pl.DeviceIdType.MESH)

    def row_arrival(e):
        return pltpu.make_async_remote_copy(
            src_ref=row.at[0], dst_ref=rows_in.at[e],
            send_sem=row_send.at[e], recv_sem=row_recv.at[e],
            device_id={"ctx": e, "ch": home}, device_id_type=pl.DeviceIdType.MESH)

    def part_copy(e):
        return pltpu.make_async_remote_copy(
            src_ref=parts_out.at[e // pieces], dst_ref=parts_in.at[me],
            send_sem=part_send.at[e], recv_sem=part_recv.at[me],
            device_id=spot(group * devs + e, groups), device_id_type=pl.DeviceIdType.MESH)

    def part_arrival(e):
        return pltpu.make_async_remote_copy(
            src_ref=parts_out.at[0], dst_ref=parts_in.at[e],
            send_sem=part_send.at[e], recv_sem=part_recv.at[e],
            device_id=spot(group * devs + e, groups), device_id_type=pl.DeviceIdType.MESH)

    def remote(condition, act):
        pl.when(jnp.logical_not(condition))(act)

    row[0] = pack_ref[chans:chans + 1, :]

    @pl.when(local)
    def _():
        rows_in[place] = pack_ref[chans:chans + 1, :]

    lane = iota((ORDER, CHUNK), 1).astype(f32)
    rest = jnp.zeros((CHUNK - ORDER, CHUNK), bf16)

    for k in range(count):
        at = pl.ds(k * CHUNK, CHUNK)
        to = pl.ds(k * rows, rows)
        xs[to, :] = input_ref[:, :, at].astype(f32).reshape(rows, CHUNK)
        mid = grad_ref[:, :, at].astype(f32) * gate_ref[:, :, at].astype(f32)
        gs[to, :] = mid.astype(bf16).astype(f32).reshape(rows, CHUNK)

    pl.semaphore_wait(barrier, everyone - 1)
    for e in range(devs):
        remote(local & (me == e), lambda e=e: row_copy(e).start())

    def pick(c):
        return pl.ds(c, count * seqs, stride=chans)

    for c in range(chans):
        x = xs[pick(c), :].astype(bf16)
        g = gs[pick(c), :].astype(bf16)
        outer = dot(x, g, TN)
        acc = jnp.zeros((8, CHUNK), f32)
        for q in range(CHUNK // 8):
            piece = outer[8 * q:8 * q + 8]
            keep = iota((8, CHUNK), 1) >= iota((8, CHUNK), 0) + 8 * q
            acc = acc + turn(jnp.where(keep, piece, 0.0), -8 * q)
        acc = skew8(acc, -1)
        lags[8 * c:8 * c + 8, :] = acc
        wl[2, c:c + 1, :] = jnp.sum(acc, axis=0, keepdims=True)

    for e in range(devs):
        remote(local & (place == e), lambda e=e: row_arrival(e).wait_recv())
    for c in range(chans):
        line = iota((1, CHUNK), 1)
        res = jnp.zeros((1, CHUNK), f32)
        rate = jnp.zeros((1, CHUNK), f32)
        for p in range(pieces):
            got = rows_in[c * pieces + p]
            keep = (line >= held * p) & (line < held * (p + 1))
            res = res + jnp.where(keep, turn(got, held * p), 0.0)
            rate = rate + jnp.where(keep, turn(got, held * p - held), 0.0)
        tabs[0, c:c + 1, :] = res
        tabs[1, c:c + 1, :] = rate
        own = iota((ORDER, CHUNK), 0) == iota((ORDER, CHUNK), 1)
        span_of = pl.ds(c * ORDER, ORDER)
        rcol = jnp.sum(jnp.where(own, jnp.broadcast_to(rate, (ORDER, CHUNK)), 0.0), axis=1, keepdims=True)
        gain = res * jnp.sqrt(2.0 * rate)
        gcol = jnp.sum(jnp.where(own, jnp.broadcast_to(gain, (ORDER, CHUNK)), 0.0), axis=1, keepdims=True)
        rcols[span_of, :] = jnp.broadcast_to(rcol, (ORDER, CHUNK))
        gcols[span_of, :] = jnp.broadcast_to(gcol, (ORDER, CHUNK))

    for c in range(chans):
        rc = rcols[c * ORDER:(c + 1) * ORDER, :]
        x = xs[pick(c), :].astype(bf16)
        g = gs[pick(c), :].astype(bf16)
        dec = jnp.exp(-rc * lane)
        eg = jnp.exp(-rc * (lane + 1.0))
        ep = jnp.exp(-rc * (CHUNK - 1.0 - lane))
        wx = jnp.concatenate([ep.astype(bf16), rest, (ep * (CHUNK - 1.0 - lane)).astype(bf16), rest], 0)
        wg = jnp.concatenate([eg.astype(bf16), rest, (eg * (lane + 1.0)).astype(bf16), rest], 0)
        wd = jnp.concatenate([dec.astype(bf16), rest, (dec * lane).astype(bf16), rest], 0)
        px = dot(x, wx, NT)
        p0[pick(c), :] = px[:, :CHUNK]
        p1[pick(c), :] = px[:, CHUNK:]
        pg = dot(g, wg, NT)
        g0[pick(c), :] = pg[:, :CHUNK]
        g1[pick(c), :] = pg[:, CHUNK:]
        acc = lags[8 * c:8 * c + 8, :]
        high = acc.astype(bf16)
        low = (acc - high.astype(f32)).astype(bf16)
        near = jnp.sum(dot(high, wd, NT) + dot(low, wd, NT), axis=0, keepdims=True)
        wl[0, c:c + 1, :] = near[:, :CHUNK]
        wl[1, c:c + 1, :] = near[:, CHUNK:]

    rl = jnp.concatenate([tabs[1]] * seqs, 0)
    fade = jnp.exp(-rl * CHUNK)
    zero = jnp.zeros((rows, CHUNK), f32)
    s0, s1, weighted, moment = zero, zero, zero, zero
    for k in range(count):
        to = pl.ds(k * rows, rows)
        a0, a1, b0, b1 = p0[to, :], p1[to, :], g0[to, :], g1[to, :]
        weighted = weighted + b0 * s0
        moment = moment + b1 * s0 + b0 * s1
        p0[to, :] = s0
        s0, s1 = fade * s0 + a0, fade * (s1 + CHUNK * s0) + a1
    r0, r1 = zero, zero
    for k in reversed(range(count)):
        to = pl.ds(k * rows, rows)
        b0, b1 = g0[to, :], g1[to, :]
        g0[to, :] = r0
        r0, r1 = fade * r0 + b0, fade * (r1 + CHUNK * r0) + b1

    def pack(v):
        total = v[0:8]
        for q in range(1, rows // 8):
            total = total + turn(v[8 * q:8 * q + 8], ORDER * q)
        return total

    def unpack(v):
        keep = iota((8, CHUNK), 1) < ORDER
        return jnp.concatenate([jnp.where(keep, turn(v, -ORDER * q), 0.0) for q in range(rows // 8)], 0)

    zeroth = jnp.where(iota((chans, CHUNK), 1) == 0, factor * wl[2], 0.0)
    skips = jnp.zeros((8, CHUNK), f32)
    for q in range(chans // 8):
        skips = skips + turn(zeroth[8 * q:8 * q + 8], ORDER * (rows // 8) + q)
    send[0] = pack(s0) + skips
    send[1] = pack(r0) + skips
    copies = []
    for d in range(1, devs):
        copy = pltpu.make_async_remote_copy(
            src_ref=send.at[(me + d) // devs],
            dst_ref=slots.at[me],
            send_sem=send_sem.at[d],
            recv_sem=recv_sem.at[d],
            device_id={"ctx": lax.rem(me + d, devs)},
            device_id_type=pl.DeviceIdType.MESH,
        )
        copy.start()
        copies.append(copy)

    for c in range(chans):
        rc = rcols[c * ORDER:(c + 1) * ORDER, :]
        gc = gcols[c * ORDER:(c + 1) * ORDER, :]
        kern = jnp.sum(gc * jnp.exp(-rc * lane), axis=0, keepdims=True)
        base = skew8(jnp.broadcast_to(kern, (8, CHUNK)), 1)
        parts = []
        for q in range(CHUNK // 8):
            keep = iota((8, CHUNK), 1) >= iota((8, CHUNK), 0) + 8 * q
            parts.append(jnp.where(keep, turn(base, 8 * q), 0.0))
        toep = jnp.concatenate(parts, 0).astype(bf16)
        x = xs[pick(c), :]
        g = gs[pick(c), :]
        sk = pack_ref[c:c + 1, :]
        ys[pick(c), :] = dot(x.astype(bf16), toep, NN) + sk * x
        zs[pick(c), :] = dot(g.astype(bf16), toep, NT) + sk * g

    for copy in copies:
        copy.wait()
    rp = pack(rl)
    s_in, sn_in, r_in = (jnp.zeros((8, CHUNK), f32) for _ in range(3))
    for d in range(1, devs):
        v = slots[lax.rem(me + devs - d, devs)]
        skips = skips + v
        left = jnp.where(me >= d, 1.0, 0.0)
        term = left * jnp.exp(-rp * (span * (d - 1.0))) * v
        s_in = s_in + term
        sn_in = sn_in + (span * (d - 1.0)) * term
        r_in = r_in + (1.0 - left) * jnp.exp(-rp * (span * (devs - d - 1.0))) * v
    s_in, sn_in, r_in = unpack(s_in), unpack(sn_in), unpack(r_in)
    weighted = weighted + r0 * s_in
    moment = moment + r1 * s_in + r0 * sn_in + s1 * r_in
    for s in range(seqs):
        wl[0] = wl[0] + weighted[s * chans:(s + 1) * chans]
        wl[1] = wl[1] + moment[s * chans:(s + 1) * chans]
    res, rate = tabs[0], tabs[1]
    scale = factor * jnp.sqrt(2.0 * rate)
    d_res = jnp.where(iota((chans, CHUNK), 1) < ORDER, scale * wl[0], 0.0)
    d_log = scale * res * (0.5 * wl[0] - rate * wl[1])
    both = d_res + turn(jnp.where(iota((chans, CHUNK), 1) < ORDER, d_log, 0.0), ORDER)
    for c in range(chans):
        parts_out[c] = both[c:c + 1, :]
    for e in range(devs):
        remote(local & (place == e), lambda e=e: part_copy(e).start())

        @pl.when(local & (place == e))
        def _(e=e):
            parts_in[me] = both[e // pieces:e // pieces + 1, :]


    for k in range(count):
        to = pl.ds(k * rows, rows)
        p0[to, :] = p0[to, :] + s_in
        s_in = s_in * fade
    for k in reversed(range(count)):
        to = pl.ds(k * rows, rows)
        g0[to, :] = g0[to, :] + r_in
        r_in = r_in * fade

    for c in range(chans):
        rc = rcols[c * ORDER:(c + 1) * ORDER, :]
        gc = gcols[c * ORDER:(c + 1) * ORDER, :]
        we = jnp.concatenate([(gc * jnp.exp(-rc * (lane + 1.0))).astype(bf16), rest], 0)
        wp = jnp.concatenate([(gc * jnp.exp(-rc * (CHUNK - 1.0 - lane))).astype(bf16), rest], 0)
        ys[pick(c), :] = ys[pick(c), :] + dot(p0[pick(c), :].astype(bf16), we, NN)
        zs[pick(c), :] = zs[pick(c), :] + dot(g0[pick(c), :].astype(bf16), wp, NN)

    for k in range(count):
        at = pl.ds(k * CHUNK, CHUNK)
        to = pl.ds(k * rows, rows)
        conv = ys[to, :].astype(bf16).astype(f32).reshape(seqs, chans, CHUNK)
        dgate_ref[:, :, at] = (grad_ref[:, :, at].astype(f32) * conv).astype(bf16)
        din_ref[:, :, at] = zs[to, :].astype(bf16).reshape(seqs, chans, CHUNK)

    for e in range(devs):
        remote(local & (me == e), lambda e=e: part_arrival(e).wait_recv())
    total = parts_in[0]
    for e in range(1, devs):
        total = total + parts_in[e]
    for e in range(devs):
        remote(local & (me == e), lambda e=e: row_copy(e).wait_send())
        remote(local & (place == e), lambda e=e: part_copy(e).wait_send())
    mine = total
    for p in range(1, pieces):
        mine = jnp.where(lax.rem(place, pieces) == p, turn(total, -held * p), mine)
    out_ref[0:8, :] = skips
    out_ref[8:16, :] = jnp.broadcast_to(mine, (8, CHUNK))


def shards(grad_out, inputs, gates, residues, rates, skip):
    seqs, chans, span = grad_out.shape
    devs = lax.axis_size("ctx")
    groups = lax.axis_size("ch")
    held = residues.shape[0]
    factor = (seqs * span * devs) ** (-0.5)
    params = jnp.pad(jnp.concatenate([residues, rates]), (0, CHUNK - 2 * held))
    packed = jnp.concatenate(
        [jnp.broadcast_to(skip[:, None], (chans, CHUNK)), jnp.broadcast_to(params[None], (8, CHUNK))], 0)
    big = pltpu.VMEM((span // CHUNK * seqs * chans, CHUNK), f32)
    line = pltpu.VMEM((chans, 1, CHUNK), f32)
    lines = pltpu.VMEM((devs, 1, CHUNK), f32)
    wide = pltpu.VMEM((chans * ORDER, CHUNK), f32)
    vmem = pl.BlockSpec(memory_space=pltpu.VMEM)
    d_input, d_gate, sums = pl.pallas_call(
        functools.partial(body, devs, groups, held, factor),
        out_shape=(
            jax.ShapeDtypeStruct(grad_out.shape, bf16),
            jax.ShapeDtypeStruct(grad_out.shape, bf16),
            jax.ShapeDtypeStruct((16, CHUNK), f32),
        ),
        in_specs=[vmem] * 4,
        out_specs=(vmem, vmem, vmem),
        scratch_shapes=[big] * 8 + [
            pltpu.VMEM((3, chans, CHUNK), f32),
            pltpu.VMEM((8 * chans, CHUNK), f32),
            wide,
            wide,
            pltpu.VMEM((2, chans, CHUNK), f32),
            pltpu.VMEM((2, 8, CHUNK), f32),
            pltpu.VMEM((devs, 8, CHUNK), f32),
            pltpu.VMEM((1, 1, CHUNK), f32),
            lines,
            line,
            lines,
        ] + [pltpu.SemaphoreType.DMA((devs,))] * 6,
        compiler_params=pltpu.CompilerParams(
            collective_id=0, has_side_effects=True, vmem_limit_bytes=40 * 2 ** 20
        ),
    )(grad_out, inputs, gates, packed)
    first = ORDER * (seqs * chans // 8)
    d_skip = sums[0:8, first:first + chans // 8].T.reshape(-1)
    return (d_input, d_gate, sums[8, :held], sums[8, ORDER:ORDER + held], d_skip)


def solution(mesh):
    wide = P(None, "ch", "ctx")
    flat = P(("ctx", "ch"))
    return jax.shard_map(
        shards,
        mesh=mesh,
        in_specs=(wide, wide, wide, flat, flat, P("ch")),
        out_specs=(wide, wide, flat, flat, P("ch")),
        check_vma=False,
    )
```

```python
import functools

import jax
import jax.numpy as jnp
from jax import lax
from jax.experimental import pallas as pl
from jax.experimental.pallas import tpu as pltpu
from jax.sharding import PartitionSpec as P

ORDER = 16
CHUNK = 128
f32 = jnp.float32
bf16 = jnp.bfloat16
NT = (((1,), (1,)), ((), ()))
TN = (((0,), (0,)), ((), ()))
NN = (((1,), (0,)), ((), ()))


def dot(a, b, dims):
    return lax.dot_general(a, b, dims, preferred_element_type=f32)


def iota(shape, axis):
    return lax.broadcasted_iota(jnp.int32, shape, axis)


def turn(v, shift):
    shift = shift % CHUNK
    return v if shift == 0 else pltpu.roll(v, shift, axis=1)


def skew8(v, sign):
    row = iota((8, CHUNK), 0)
    for bit in (1, 2, 4):
        v = jnp.where((row // bit) % 2 == 1, turn(v, sign * bit), v)
    return v


def spot(flat, groups):
    return {"ctx": flat // groups, "ch": lax.rem(flat, groups)}


def body(devs, groups, held, factor, grad_hbm, input_hbm, gate_hbm, res_hbm, rate_hbm, skip_hbm,
         din_ref, dgate_ref, out_ref,
         xs, gs, p0, p1, g0, g1, ys, zs, wl, lags, rcols, gcols, tabs, send, slots,
         row, rows_in, parts_out, parts_in,
         grad_ref, input_ref, gate_ref, res_ref, rate_ref, skip_ref, gains, in_sem,
         send_sem, recv_sem, row_send, row_recv, part_send, part_recv):
    loads = [pltpu.make_async_copy(a, b, in_sem.at[q]) for q, (a, b) in enumerate((
        (res_hbm, res_ref), (rate_hbm, rate_ref), (skip_hbm, skip_ref),
        (grad_hbm, grad_ref), (gate_hbm, gate_ref), (input_hbm, input_ref)))]
    for load in loads:
        load.start()
    seqs, chans, span = grad_ref.shape
    rows = seqs * chans
    count = span // CHUNK
    me = lax.axis_index("ctx")
    group = lax.axis_index("ch")
    flat = me * groups + group
    everyone = devs * groups
    home = flat // devs
    place = lax.rem(flat, devs)
    local = home == group
    pieces = ORDER // held
    barrier = pltpu.get_barrier_semaphore()

    @pl.loop(1, everyone)
    def _(d):
        pl.semaphore_signal(barrier, inc=1, device_id=spot(lax.rem(flat + d, everyone), groups),
                            device_id_type=pl.DeviceIdType.MESH)

    def row_copy(e):
        return pltpu.make_async_remote_copy(
            src_ref=row.at[0], dst_ref=rows_in.at[place],
            send_sem=row_send.at[e], recv_sem=row_recv.at[place],
            device_id={"ctx": e, "ch": home}, device_id_type=pl.DeviceIdType.MESH)

    def row_arrival(e):
        return pltpu.make_async_remote_copy(
            src_ref=row.at[0], dst_ref=rows_in.at[e],
            send_sem=row_send.at[e], recv_sem=row_recv.at[e],
            device_id={"ctx": e, "ch": home}, device_id_type=pl.DeviceIdType.MESH)

    def part_copy(e):
        return pltpu.make_async_remote_copy(
            src_ref=parts_out.at[e // pieces], dst_ref=parts_in.at[me],
            send_sem=part_send.at[e], recv_sem=part_recv.at[me],
            device_id=spot(group * devs + e, groups), device_id_type=pl.DeviceIdType.MESH)

    def part_arrival(e):
        return pltpu.make_async_remote_copy(
            src_ref=parts_out.at[0], dst_ref=parts_in.at[e],
            send_sem=part_send.at[e], recv_sem=part_recv.at[e],
            device_id=spot(group * devs + e, groups), device_id_type=pl.DeviceIdType.MESH)

    def remote(condition, act):
        pl.when(jnp.logical_not(condition))(act)

    for load in loads[:3]:
        load.wait()
    packed = jnp.concatenate(
        [res_ref[...], rate_ref[...], jnp.zeros((1, CHUNK - 2 * held), f32)], axis=1)
    row[0] = packed

    @pl.when(local)
    def _():
        rows_in[place] = packed

    pl.semaphore_wait(barrier, everyone - 1)
    for e in range(devs):
        remote(local & (me == e), lambda e=e: row_copy(e).start())
    padded = jnp.concatenate([skip_ref[...], jnp.zeros((1, CHUNK - chans), f32)], axis=1)
    diagonal = iota((chans, CHUNK), 0) == iota((chans, CHUNK), 1)
    gains[...] = jnp.broadcast_to(jnp.sum(
        jnp.where(diagonal, jnp.broadcast_to(padded, (chans, CHUNK)), 0.0), axis=1, keepdims=True), (chans, CHUNK))
    for load in loads[3:]:
        load.wait()

    lane = iota((ORDER, CHUNK), 1).astype(f32)
    rest = jnp.zeros((CHUNK - ORDER, CHUNK), bf16)

    for k in range(count):
        at = pl.ds(k * CHUNK, CHUNK)
        to = pl.ds(k * rows, rows)
        xs[to, :] = input_ref[:, :, at].astype(f32).reshape(rows, CHUNK)
        mid = grad_ref[:, :, at].astype(f32) * gate_ref[:, :, at].astype(f32)
        gs[to, :] = mid.astype(bf16).astype(f32).reshape(rows, CHUNK)

    def pick(c):
        return pl.ds(c, count * seqs, stride=chans)

    for c in range(chans):
        x = xs[pick(c), :].astype(bf16)
        g = gs[pick(c), :].astype(bf16)
        outer = dot(x, g, TN)
        acc = jnp.zeros((8, CHUNK), f32)
        for q in range(CHUNK // 8):
            piece = outer[8 * q:8 * q + 8]
            keep = iota((8, CHUNK), 1) >= iota((8, CHUNK), 0) + 8 * q
            acc = acc + turn(jnp.where(keep, piece, 0.0), -8 * q)
        acc = skew8(acc, -1)
        lags[8 * c:8 * c + 8, :] = acc
        wl[2, c:c + 1, :] = jnp.sum(acc, axis=0, keepdims=True)

    for e in range(devs):
        remote(local & (place == e), lambda e=e: row_arrival(e).wait_recv())
    for c in range(chans):
        line = iota((1, CHUNK), 1)
        res = jnp.zeros((1, CHUNK), f32)
        rate = jnp.zeros((1, CHUNK), f32)
        for p in range(pieces):
            got = rows_in[c * pieces + p]
            keep = (line >= held * p) & (line < held * (p + 1))
            res = res + jnp.where(keep, turn(got, held * p), 0.0)
            rate = rate + jnp.where(keep, turn(got, held * p - held), 0.0)
        tabs[0, c:c + 1, :] = res
        tabs[1, c:c + 1, :] = rate
        own = iota((ORDER, CHUNK), 0) == iota((ORDER, CHUNK), 1)
        span_of = pl.ds(c * ORDER, ORDER)
        rcol = jnp.sum(jnp.where(own, jnp.broadcast_to(rate, (ORDER, CHUNK)), 0.0), axis=1, keepdims=True)
        gain = res * jnp.sqrt(2.0 * rate)
        gcol = jnp.sum(jnp.where(own, jnp.broadcast_to(gain, (ORDER, CHUNK)), 0.0), axis=1, keepdims=True)
        rcols[span_of, :] = jnp.broadcast_to(rcol, (ORDER, CHUNK))
        gcols[span_of, :] = jnp.broadcast_to(gcol, (ORDER, CHUNK))

    for c in range(chans):
        rc = rcols[c * ORDER:(c + 1) * ORDER, :]
        x = xs[pick(c), :].astype(bf16)
        g = gs[pick(c), :].astype(bf16)
        dec = jnp.exp(-rc * lane)
        eg = jnp.exp(-rc * (lane + 1.0))
        ep = jnp.exp(-rc * (CHUNK - 1.0 - lane))
        wx = jnp.concatenate([ep.astype(bf16), rest, (ep * (CHUNK - 1.0 - lane)).astype(bf16), rest], 0)
        wg = jnp.concatenate([eg.astype(bf16), rest, (eg * (lane + 1.0)).astype(bf16), rest], 0)
        wd = jnp.concatenate([dec.astype(bf16), rest, (dec * lane).astype(bf16), rest], 0)
        px = dot(x, wx, NT)
        p0[pick(c), :] = px[:, :CHUNK]
        p1[pick(c), :] = px[:, CHUNK:]
        pg = dot(g, wg, NT)
        g0[pick(c), :] = pg[:, :CHUNK]
        g1[pick(c), :] = pg[:, CHUNK:]
        acc = lags[8 * c:8 * c + 8, :]
        high = acc.astype(bf16)
        low = (acc - high.astype(f32)).astype(bf16)
        near = jnp.sum(dot(high, wd, NT) + dot(low, wd, NT), axis=0, keepdims=True)
        wl[0, c:c + 1, :] = near[:, :CHUNK]
        wl[1, c:c + 1, :] = near[:, CHUNK:]

    rl = jnp.concatenate([tabs[1]] * seqs, 0)
    fade = jnp.exp(-rl * CHUNK)
    zero = jnp.zeros((rows, CHUNK), f32)
    s0, s1, weighted, moment = zero, zero, zero, zero
    for k in range(count):
        to = pl.ds(k * rows, rows)
        a0, a1, b0, b1 = p0[to, :], p1[to, :], g0[to, :], g1[to, :]
        weighted = weighted + b0 * s0
        moment = moment + b1 * s0 + b0 * s1
        p0[to, :] = s0
        s0, s1 = fade * s0 + a0, fade * (s1 + CHUNK * s0) + a1
    r0, r1 = zero, zero
    for k in reversed(range(count)):
        to = pl.ds(k * rows, rows)
        b0, b1 = g0[to, :], g1[to, :]
        g0[to, :] = r0
        r0, r1 = fade * r0 + b0, fade * (r1 + CHUNK * r0) + b1

    def pack(v):
        total = v[0:8]
        for q in range(1, rows // 8):
            total = total + turn(v[8 * q:8 * q + 8], ORDER * q)
        return total

    def unpack(v):
        keep = iota((8, CHUNK), 1) < ORDER
        return jnp.concatenate([jnp.where(keep, turn(v, -ORDER * q), 0.0) for q in range(rows // 8)], 0)

    zeroth = jnp.where(iota((chans, CHUNK), 1) == 0, factor * wl[2], 0.0)
    skips = jnp.zeros((8, CHUNK), f32)
    for q in range(chans // 8):
        skips = skips + turn(zeroth[8 * q:8 * q + 8], ORDER * (rows // 8) + q)
    send[0] = pack(s0) + skips
    send[1] = pack(r0) + skips
    copies = []
    for d in range(1, devs):
        copy = pltpu.make_async_remote_copy(
            src_ref=send.at[(me + d) // devs],
            dst_ref=slots.at[me],
            send_sem=send_sem.at[d],
            recv_sem=recv_sem.at[d],
            device_id={"ctx": lax.rem(me + d, devs)},
            device_id_type=pl.DeviceIdType.MESH,
        )
        copy.start()
        copies.append(copy)

    for c in range(chans):
        rc = rcols[c * ORDER:(c + 1) * ORDER, :]
        gc = gcols[c * ORDER:(c + 1) * ORDER, :]
        kern = jnp.sum(gc * jnp.exp(-rc * lane), axis=0, keepdims=True)
        base = skew8(jnp.broadcast_to(kern, (8, CHUNK)), 1)
        parts = []
        for q in range(CHUNK // 8):
            keep = iota((8, CHUNK), 1) >= iota((8, CHUNK), 0) + 8 * q
            parts.append(jnp.where(keep, turn(base, 8 * q), 0.0))
        toep = jnp.concatenate(parts, 0).astype(bf16)
        x = xs[pick(c), :]
        g = gs[pick(c), :]
        sk = gains[c:c + 1, :]
        ys[pick(c), :] = dot(x.astype(bf16), toep, NN) + sk * x
        zs[pick(c), :] = dot(g.astype(bf16), toep, NT) + sk * g

    for copy in copies:
        copy.wait()
    rp = pack(rl)
    s_in, sn_in, r_in = (jnp.zeros((8, CHUNK), f32) for _ in range(3))
    for d in range(1, devs):
        v = slots[lax.rem(me + devs - d, devs)]
        skips = skips + v
        left = jnp.where(me >= d, 1.0, 0.0)
        term = left * jnp.exp(-rp * (span * (d - 1.0))) * v
        s_in = s_in + term
        sn_in = sn_in + (span * (d - 1.0)) * term
        r_in = r_in + (1.0 - left) * jnp.exp(-rp * (span * (devs - d - 1.0))) * v
    s_in, sn_in, r_in = unpack(s_in), unpack(sn_in), unpack(r_in)
    weighted = weighted + r0 * s_in
    moment = moment + r1 * s_in + r0 * sn_in + s1 * r_in
    for s in range(seqs):
        wl[0] = wl[0] + weighted[s * chans:(s + 1) * chans]
        wl[1] = wl[1] + moment[s * chans:(s + 1) * chans]
    res, rate = tabs[0], tabs[1]
    scale = factor * jnp.sqrt(2.0 * rate)
    d_res = jnp.where(iota((chans, CHUNK), 1) < ORDER, scale * wl[0], 0.0)
    d_log = scale * res * (0.5 * wl[0] - rate * wl[1])
    both = d_res + turn(jnp.where(iota((chans, CHUNK), 1) < ORDER, d_log, 0.0), ORDER)
    for c in range(chans):
        parts_out[c] = both[c:c + 1, :]
    for e in range(devs):
        remote(local & (place == e), lambda e=e: part_copy(e).start())

        @pl.when(local & (place == e))
        def _(e=e):
            parts_in[me] = both[e // pieces:e // pieces + 1, :]


    for k in range(count):
        to = pl.ds(k * rows, rows)
        p0[to, :] = p0[to, :] + s_in
        s_in = s_in * fade
    for k in reversed(range(count)):
        to = pl.ds(k * rows, rows)
        g0[to, :] = g0[to, :] + r_in
        r_in = r_in * fade

    for c in range(chans):
        rc = rcols[c * ORDER:(c + 1) * ORDER, :]
        gc = gcols[c * ORDER:(c + 1) * ORDER, :]
        we = jnp.concatenate([(gc * jnp.exp(-rc * (lane + 1.0))).astype(bf16), rest], 0)
        wp = jnp.concatenate([(gc * jnp.exp(-rc * (CHUNK - 1.0 - lane))).astype(bf16), rest], 0)
        ys[pick(c), :] = ys[pick(c), :] + dot(p0[pick(c), :].astype(bf16), we, NN)
        zs[pick(c), :] = zs[pick(c), :] + dot(g0[pick(c), :].astype(bf16), wp, NN)

    for k in range(count):
        at = pl.ds(k * CHUNK, CHUNK)
        to = pl.ds(k * rows, rows)
        conv = ys[to, :].astype(bf16).astype(f32).reshape(seqs, chans, CHUNK)
        dgate_ref[:, :, at] = (grad_ref[:, :, at].astype(f32) * conv).astype(bf16)
        din_ref[:, :, at] = zs[to, :].astype(bf16).reshape(seqs, chans, CHUNK)

    for e in range(devs):
        remote(local & (me == e), lambda e=e: part_arrival(e).wait_recv())
    total = parts_in[0]
    for e in range(1, devs):
        total = total + parts_in[e]
    for e in range(devs):
        remote(local & (me == e), lambda e=e: row_copy(e).wait_send())
        remote(local & (place == e), lambda e=e: part_copy(e).wait_send())
    mine = total
    for p in range(1, pieces):
        mine = jnp.where(lax.rem(place, pieces) == p, turn(total, -held * p), mine)
    first = ORDER * (rows // 8)
    spread = jnp.zeros((8, CHUNK), f32)
    for q in range(chans // 8):
        column = jnp.sum(jnp.where(iota((8, CHUNK), 1) == first + q, skips, 0.0), axis=1, keepdims=True)
        spread = spread + jnp.where(iota((8, CHUNK), 1) == iota((8, CHUNK), 0) + 8 * q, column, 0.0)
    out_ref[0:8, :] = jnp.broadcast_to(jnp.sum(spread, axis=0, keepdims=True), (8, CHUNK))
    out_ref[8:16, :] = jnp.broadcast_to(mine, (8, CHUNK))


def shards(grad_out, inputs, gates, residues, rates, skip):
    seqs, chans, span = grad_out.shape
    devs = lax.axis_size("ctx")
    groups = lax.axis_size("ch")
    held = residues.shape[0]
    factor = (seqs * span * devs) ** (-0.5)
    big = pltpu.VMEM((span // CHUNK * seqs * chans, CHUNK), f32)
    line = pltpu.VMEM((chans, 1, CHUNK), f32)
    lines = pltpu.VMEM((devs, 1, CHUNK), f32)
    wide = pltpu.VMEM((chans * ORDER, CHUNK), f32)
    vmem = pl.BlockSpec(memory_space=pltpu.VMEM)
    d_input, d_gate, sums = pl.pallas_call(
        functools.partial(body, devs, groups, held, factor),
        out_shape=(
            jax.ShapeDtypeStruct(grad_out.shape, bf16),
            jax.ShapeDtypeStruct(grad_out.shape, bf16),
            jax.ShapeDtypeStruct((16, CHUNK), f32),
        ),
        in_specs=[pl.BlockSpec(memory_space=pltpu.HBM)] * 6,
        out_specs=(vmem, vmem, vmem),
        scratch_shapes=[big] * 8 + [
            pltpu.VMEM((3, chans, CHUNK), f32),
            pltpu.VMEM((8 * chans, CHUNK), f32),
            wide,
            wide,
            pltpu.VMEM((2, chans, CHUNK), f32),
            pltpu.VMEM((2, 8, CHUNK), f32),
            pltpu.VMEM((devs, 8, CHUNK), f32),
            pltpu.VMEM((1, 1, CHUNK), f32),
            lines,
            line,
            lines,
            pltpu.VMEM(grad_out.shape, bf16),
            pltpu.VMEM(grad_out.shape, bf16),
            pltpu.VMEM(grad_out.shape, bf16),
            pltpu.VMEM((1, held), f32),
            pltpu.VMEM((1, held), f32),
            pltpu.VMEM((1, chans), f32),
            pltpu.VMEM((chans, CHUNK), f32),
            pltpu.SemaphoreType.DMA((6,)),
        ] + [pltpu.SemaphoreType.DMA((devs,))] * 6,
        compiler_params=pltpu.CompilerParams(
            collective_id=0, has_side_effects=True, vmem_limit_bytes=40 * 2 ** 20
        ),
    )(grad_out, inputs, gates, residues.reshape(1, -1), rates.reshape(1, -1), skip.reshape(1, -1))
    return (d_input, d_gate, sums[8, :held], sums[8, ORDER:ORDER + held], sums[0, :chans])


def solution(mesh):
    wide = P(None, "ch", "ctx")
    flat = P(("ctx", "ch"))
    return jax.shard_map(
        shards,
        mesh=mesh,
        in_specs=(wide, wide, wide, flat, flat, P("ch")),
        out_specs=(wide, wide, flat, flat, P("ch")),
        check_vma=False,
    )
```

```python
import functools

import jax
import jax.numpy as jnp
from jax import lax
from jax.experimental import pallas as pl
from jax.experimental.pallas import tpu as pltpu
from jax.sharding import PartitionSpec as P

ORDER = 16
CHUNK = 128
f32 = jnp.float32
bf16 = jnp.bfloat16
NT = (((1,), (1,)), ((), ()))
TN = (((0,), (0,)), ((), ()))
NN = (((1,), (0,)), ((), ()))


def dot(a, b, dims):
    return lax.dot_general(a, b, dims, preferred_element_type=f32)


def iota(shape, axis):
    return lax.broadcasted_iota(jnp.int32, shape, axis)


def turn(v, shift):
    shift = shift % CHUNK
    return v if shift == 0 else pltpu.roll(v, shift, axis=1)


def skew8(v, sign):
    row = iota((8, CHUNK), 0)
    for bit in (1, 2, 4):
        v = jnp.where((row // bit) % 2 == 1, turn(v, sign * bit), v)
    return v


def spot(flat, groups):
    return {"ctx": flat // groups, "ch": lax.rem(flat, groups)}


def body(devs, groups, held, factor, grad_hbm, input_hbm, gate_hbm, res_hbm, rate_hbm, skip_hbm,
         din_ref, dgate_ref, out_ref,
         xs, gs, p0, p1, g0, g1, ys, zs, wl, lags, rcols, gcols, tabs, send, slots,
         row, rows_in, parts_out, parts_in,
         grad_ref, input_ref, gate_ref, res_ref, rate_ref, skip_ref, gains, in_sem,
         send_sem, recv_sem, row_send, row_recv, part_send, part_recv):
    loads = [pltpu.make_async_copy(a, b, in_sem.at[q]) for q, (a, b) in enumerate((
        (res_hbm, res_ref), (rate_hbm, rate_ref), (skip_hbm, skip_ref),
        (grad_hbm, grad_ref), (gate_hbm, gate_ref), (input_hbm, input_ref)))]
    for load in loads:
        load.start()
    seqs, chans, span = grad_ref.shape
    rows = seqs * chans
    count = span // CHUNK
    me = lax.axis_index("ctx")
    group = lax.axis_index("ch")
    flat = me * groups + group
    everyone = devs * groups
    home = flat // devs
    place = lax.rem(flat, devs)
    local = home == group
    pieces = ORDER // held
    barrier = pltpu.get_barrier_semaphore()

    @pl.loop(1, everyone)
    def _(d):
        pl.semaphore_signal(barrier, inc=1, device_id=spot(lax.rem(flat + d, everyone), groups),
                            device_id_type=pl.DeviceIdType.MESH)

    def row_copy(e):
        return pltpu.make_async_remote_copy(
            src_ref=row.at[0], dst_ref=rows_in.at[place],
            send_sem=row_send.at[e], recv_sem=row_recv.at[place],
            device_id={"ctx": e, "ch": home}, device_id_type=pl.DeviceIdType.MESH)

    def row_arrival(e):
        return pltpu.make_async_remote_copy(
            src_ref=row.at[0], dst_ref=rows_in.at[e],
            send_sem=row_send.at[e], recv_sem=row_recv.at[e],
            device_id={"ctx": e, "ch": home}, device_id_type=pl.DeviceIdType.MESH)

    def part_copy(e):
        return pltpu.make_async_remote_copy(
            src_ref=parts_out.at[e // pieces], dst_ref=parts_in.at[me],
            send_sem=part_send.at[e], recv_sem=part_recv.at[me],
            device_id=spot(group * devs + e, groups), device_id_type=pl.DeviceIdType.MESH)

    def part_arrival(e):
        return pltpu.make_async_remote_copy(
            src_ref=parts_out.at[0], dst_ref=parts_in.at[e],
            send_sem=part_send.at[e], recv_sem=part_recv.at[e],
            device_id=spot(group * devs + e, groups), device_id_type=pl.DeviceIdType.MESH)

    def remote(condition, act):
        pl.when(jnp.logical_not(condition))(act)

    for load in loads[:3]:
        load.wait()
    packed = jnp.concatenate(
        [res_ref[...], rate_ref[...], jnp.zeros((1, CHUNK - 2 * held), f32)], axis=1)
    row[0] = packed

    @pl.when(local)
    def _():
        rows_in[place] = packed

    pl.semaphore_wait(barrier, everyone - 1)
    for e in range(devs):
        remote(local & (me == e), lambda e=e: row_copy(e).start())
    padded = jnp.concatenate([skip_ref[...], jnp.zeros((1, CHUNK - chans), f32)], axis=1)
    diagonal = iota((chans, CHUNK), 0) == iota((chans, CHUNK), 1)
    gains[...] = jnp.broadcast_to(jnp.sum(
        jnp.where(diagonal, jnp.broadcast_to(padded, (chans, CHUNK)), 0.0), axis=1, keepdims=True), (chans, CHUNK))
    for load in loads[3:]:
        load.wait()

    lane = iota((ORDER, CHUNK), 1).astype(f32)
    rest = jnp.zeros((CHUNK - ORDER, CHUNK), bf16)

    for k in range(count):
        at = pl.ds(k * CHUNK, CHUNK)
        to = pl.ds(k * rows, rows)
        xs[to, :] = input_ref[:, :, at].astype(f32).reshape(rows, CHUNK)
        mid = grad_ref[:, :, at].astype(f32) * gate_ref[:, :, at].astype(f32)
        gs[to, :] = mid.astype(bf16).astype(f32).reshape(rows, CHUNK)

    def pick(c):
        return pl.ds(c, count * seqs, stride=chans)

    for c in range(chans):
        x = xs[pick(c), :].astype(bf16)
        g = gs[pick(c), :].astype(bf16)
        outer = dot(x, g, TN)
        acc = jnp.zeros((8, CHUNK), f32)
        for q in range(CHUNK // 8):
            piece = outer[8 * q:8 * q + 8]
            keep = iota((8, CHUNK), 1) >= iota((8, CHUNK), 0) + 8 * q
            acc = acc + turn(jnp.where(keep, piece, 0.0), -8 * q)
        acc = skew8(acc, -1)
        lags[8 * c:8 * c + 8, :] = acc
        wl[2, c:c + 1, :] = jnp.sum(acc, axis=0, keepdims=True)

    for e in range(devs):
        remote(local & (place == e), lambda e=e: row_arrival(e).wait_recv())
    for c in range(chans):
        line = iota((1, CHUNK), 1)
        res = jnp.zeros((1, CHUNK), f32)
        rate = jnp.zeros((1, CHUNK), f32)
        for p in range(pieces):
            got = rows_in[c * pieces + p]
            keep = (line >= held * p) & (line < held * (p + 1))
            res = res + jnp.where(keep, turn(got, held * p), 0.0)
            rate = rate + jnp.where(keep, turn(got, held * p - held), 0.0)
        tabs[0, c:c + 1, :] = res
        tabs[1, c:c + 1, :] = rate
        own = iota((ORDER, CHUNK), 0) == iota((ORDER, CHUNK), 1)
        span_of = pl.ds(c * ORDER, ORDER)
        rcol = jnp.sum(jnp.where(own, jnp.broadcast_to(rate, (ORDER, CHUNK)), 0.0), axis=1, keepdims=True)
        gain = res * jnp.sqrt(2.0 * rate)
        gcol = jnp.sum(jnp.where(own, jnp.broadcast_to(gain, (ORDER, CHUNK)), 0.0), axis=1, keepdims=True)
        rcols[span_of, :] = jnp.broadcast_to(rcol, (ORDER, CHUNK))
        gcols[span_of, :] = jnp.broadcast_to(gcol, (ORDER, CHUNK))

    for c in range(chans):
        rc = rcols[c * ORDER:(c + 1) * ORDER, :]
        x = xs[pick(c), :].astype(bf16)
        g = gs[pick(c), :].astype(bf16)
        dec = jnp.exp(-rc * lane)
        eg = jnp.exp(-rc * (lane + 1.0))
        ep = jnp.exp(-rc * (CHUNK - 1.0 - lane))
        wx = jnp.concatenate([ep.astype(bf16), rest, (ep * (CHUNK - 1.0 - lane)).astype(bf16), rest], 0)
        wg = jnp.concatenate([eg.astype(bf16), rest, (eg * (lane + 1.0)).astype(bf16), rest], 0)
        wd = jnp.concatenate([dec.astype(bf16), rest, (dec * lane).astype(bf16), rest], 0)
        px = dot(x, wx, NT)
        p0[pick(c), :] = px[:, :CHUNK]
        p1[pick(c), :] = px[:, CHUNK:]
        pg = dot(g, wg, NT)
        g0[pick(c), :] = pg[:, :CHUNK]
        g1[pick(c), :] = pg[:, CHUNK:]
        acc = lags[8 * c:8 * c + 8, :]
        high = acc.astype(bf16)
        low = (acc - high.astype(f32)).astype(bf16)
        near = jnp.sum(dot(high, wd, NT) + dot(low, wd, NT), axis=0, keepdims=True)
        wl[0, c:c + 1, :] = near[:, :CHUNK]
        wl[1, c:c + 1, :] = near[:, CHUNK:]

    rl = jnp.concatenate([tabs[1]] * seqs, 0)
    fade = jnp.exp(-rl * CHUNK)
    zero = jnp.zeros((rows, CHUNK), f32)
    s0, s1, weighted, moment = zero, zero, zero, zero
    for k in range(count):
        to = pl.ds(k * rows, rows)
        a0, a1, b0, b1 = p0[to, :], p1[to, :], g0[to, :], g1[to, :]
        weighted = weighted + b0 * s0
        moment = moment + b1 * s0 + b0 * s1
        p0[to, :] = s0
        s0, s1 = fade * s0 + a0, fade * (s1 + CHUNK * s0) + a1
    r0, r1 = zero, zero
    for k in reversed(range(count)):
        to = pl.ds(k * rows, rows)
        b0, b1 = g0[to, :], g1[to, :]
        g0[to, :] = r0
        r0, r1 = fade * r0 + b0, fade * (r1 + CHUNK * r0) + b1

    def pack(v):
        total = v[0:8]
        for q in range(1, rows // 8):
            total = total + turn(v[8 * q:8 * q + 8], ORDER * q)
        return total

    def unpack(v):
        keep = iota((8, CHUNK), 1) < ORDER
        return jnp.concatenate([jnp.where(keep, turn(v, -ORDER * q), 0.0) for q in range(rows // 8)], 0)

    zeroth = jnp.where(iota((chans, CHUNK), 1) == 0, factor * wl[2], 0.0)
    skips = jnp.zeros((8, CHUNK), f32)
    for q in range(chans // 8):
        skips = skips + turn(zeroth[8 * q:8 * q + 8], ORDER * (rows // 8) + q)
    send[0] = pack(s0) + skips
    send[1] = pack(r0) + skips
    copies = []
    for d in range(1, devs):
        copy = pltpu.make_async_remote_copy(
            src_ref=send.at[(me + d) // devs],
            dst_ref=slots.at[me],
            send_sem=send_sem.at[d],
            recv_sem=recv_sem.at[d],
            device_id={"ctx": lax.rem(me + d, devs)},
            device_id_type=pl.DeviceIdType.MESH,
        )
        copy.start()
        copies.append(copy)

    for c in range(chans):
        rc = rcols[c * ORDER:(c + 1) * ORDER, :]
        gc = gcols[c * ORDER:(c + 1) * ORDER, :]
        kern = jnp.sum(gc * jnp.exp(-rc * lane), axis=0, keepdims=True)
        base = skew8(jnp.broadcast_to(kern, (8, CHUNK)), 1)
        parts = []
        for q in range(CHUNK // 8):
            keep = iota((8, CHUNK), 1) >= iota((8, CHUNK), 0) + 8 * q
            parts.append(jnp.where(keep, turn(base, 8 * q), 0.0))
        toep = jnp.concatenate(parts, 0).astype(bf16)
        x = xs[pick(c), :]
        g = gs[pick(c), :]
        sk = gains[c:c + 1, :]
        ys[pick(c), :] = dot(x.astype(bf16), toep, NN) + sk * x
        zs[pick(c), :] = dot(g.astype(bf16), toep, NT) + sk * g

    for copy in copies:
        copy.wait()
    rp = pack(rl)
    s_in, sn_in, r_in = (jnp.zeros((8, CHUNK), f32) for _ in range(3))
    for d in range(1, devs):
        v = slots[lax.rem(me + devs - d, devs)]
        skips = skips + v
        left = jnp.where(me >= d, 1.0, 0.0)
        term = left * jnp.exp(-rp * (span * (d - 1.0))) * v
        s_in = s_in + term
        sn_in = sn_in + (span * (d - 1.0)) * term
        r_in = r_in + (1.0 - left) * jnp.exp(-rp * (span * (devs - d - 1.0))) * v
    s_in, sn_in, r_in = unpack(s_in), unpack(sn_in), unpack(r_in)
    weighted = weighted + r0 * s_in
    moment = moment + r1 * s_in + r0 * sn_in + s1 * r_in
    for s in range(seqs):
        wl[0] = wl[0] + weighted[s * chans:(s + 1) * chans]
        wl[1] = wl[1] + moment[s * chans:(s + 1) * chans]
    res, rate = tabs[0], tabs[1]
    scale = factor * jnp.sqrt(2.0 * rate)
    d_res = jnp.where(iota((chans, CHUNK), 1) < ORDER, scale * wl[0], 0.0)
    d_log = scale * res * (0.5 * wl[0] - rate * wl[1])
    both = d_res + turn(jnp.where(iota((chans, CHUNK), 1) < ORDER, d_log, 0.0), ORDER)
    for c in range(chans):
        parts_out[c] = both[c:c + 1, :]
    for e in range(devs):
        remote(local & (place == e), lambda e=e: part_copy(e).start())

        @pl.when(local & (place == e))
        def _(e=e):
            parts_in[me] = both[e // pieces:e // pieces + 1, :]


    for k in range(count):
        to = pl.ds(k * rows, rows)
        p0[to, :] = p0[to, :] + s_in
        s_in = s_in * fade
    for k in reversed(range(count)):
        to = pl.ds(k * rows, rows)
        g0[to, :] = g0[to, :] + r_in
        r_in = r_in * fade

    for c in range(chans):
        rc = rcols[c * ORDER:(c + 1) * ORDER, :]
        gc = gcols[c * ORDER:(c + 1) * ORDER, :]
        we = jnp.concatenate([(gc * jnp.exp(-rc * (lane + 1.0))).astype(bf16), rest], 0)
        wp = jnp.concatenate([(gc * jnp.exp(-rc * (CHUNK - 1.0 - lane))).astype(bf16), rest], 0)
        ys[pick(c), :] = ys[pick(c), :] + dot(p0[pick(c), :].astype(bf16), we, NN)
        zs[pick(c), :] = zs[pick(c), :] + dot(g0[pick(c), :].astype(bf16), wp, NN)

    for k in range(count):
        at = pl.ds(k * CHUNK, CHUNK)
        to = pl.ds(k * rows, rows)
        conv = ys[to, :].astype(bf16).astype(f32).reshape(seqs, chans, CHUNK)
        dgate_ref[:, :, at] = (grad_ref[:, :, at].astype(f32) * conv).astype(bf16)
        din_ref[:, :, at] = zs[to, :].astype(bf16).reshape(seqs, chans, CHUNK)

    for e in range(devs):
        remote(local & (me == e), lambda e=e: part_arrival(e).wait_recv())
    total = parts_in[0]
    for e in range(1, devs):
        total = total + parts_in[e]
    for e in range(devs):
        remote(local & (me == e), lambda e=e: row_copy(e).wait_send())
        remote(local & (place == e), lambda e=e: part_copy(e).wait_send())
    mine = total
    for p in range(1, pieces):
        mine = jnp.where(lax.rem(place, pieces) == p, turn(total, -held * p), mine)
    first = ORDER * (rows // 8)
    spread = jnp.zeros((8, CHUNK), f32)
    for q in range(chans // 8):
        column = jnp.sum(jnp.where(iota((8, CHUNK), 1) == first + q, skips, 0.0), axis=1, keepdims=True)
        spread = spread + jnp.where(iota((8, CHUNK), 1) == iota((8, CHUNK), 0) + 8 * q, column, 0.0)
    out_ref[0:8, :] = jnp.broadcast_to(jnp.sum(spread, axis=0, keepdims=True), (8, CHUNK))
    out_ref[8:16, :] = jnp.broadcast_to(mine, (8, CHUNK))


def shards(grad_out, inputs, gates, residues, rates, skip):
    seqs, chans, span = grad_out.shape
    devs = lax.axis_size("ctx")
    groups = lax.axis_size("ch")
    held = residues.shape[0]
    factor = (seqs * span * devs) ** (-0.5)
    big = pltpu.VMEM((span // CHUNK * seqs * chans, CHUNK), f32)
    line = pltpu.VMEM((chans, 1, CHUNK), f32)
    lines = pltpu.VMEM((devs, 1, CHUNK), f32)
    wide = pltpu.VMEM((chans * ORDER, CHUNK), f32)
    vmem = pl.BlockSpec(memory_space=pltpu.VMEM)
    d_input, d_gate, sums = pl.pallas_call(
        functools.partial(body, devs, groups, held, factor),
        out_shape=(
            jax.ShapeDtypeStruct(grad_out.shape, bf16),
            jax.ShapeDtypeStruct(grad_out.shape, bf16),
            jax.ShapeDtypeStruct((16, CHUNK), f32),
        ),
        in_specs=[pl.BlockSpec(memory_space=pltpu.HBM)] * 6,
        out_specs=(vmem, vmem, vmem),
        scratch_shapes=[big] * 8 + [
            pltpu.VMEM((3, chans, CHUNK), f32),
            pltpu.VMEM((8 * chans, CHUNK), f32),
            wide,
            wide,
            pltpu.VMEM((2, chans, CHUNK), f32),
            pltpu.VMEM((2, 8, CHUNK), f32),
            pltpu.VMEM((devs, 8, CHUNK), f32),
            pltpu.VMEM((1, 1, CHUNK), f32),
            lines,
            line,
            lines,
            pltpu.VMEM(grad_out.shape, bf16),
            pltpu.VMEM(grad_out.shape, bf16),
            pltpu.VMEM(grad_out.shape, bf16),
            pltpu.VMEM((1, held), f32),
            pltpu.VMEM((1, held), f32),
            pltpu.VMEM((1, chans), f32),
            pltpu.VMEM((chans, CHUNK), f32),
            pltpu.SemaphoreType.DMA((6,)),
        ] + [pltpu.SemaphoreType.DMA((devs,))] * 6,
        compiler_params=pltpu.CompilerParams(
            collective_id=0, has_side_effects=True, vmem_limit_bytes=67108864
        ),
    )(grad_out, inputs, gates, residues.reshape(1, -1), rates.reshape(1, -1), skip.reshape(1, -1))
    return (d_input, d_gate, sums[8, :held], sums[8, ORDER:ORDER + held], sums[0, :chans])


def solution(mesh):
    wide = P(None, "ch", "ctx")
    flat = P(("ctx", "ch"))
    return jax.shard_map(
        shards,
        mesh=mesh,
        in_specs=(wide, wide, wide, flat, flat, P("ch")),
        out_specs=(wide, wide, flat, flat, P("ch")),
        check_vma=False,
    )
```
